512 devices in a mesh: kgrp: 16 (over x_lo, y), ga: 32 (over z, x_hi, core).
Axes of the slice: x: 4 (x_hi: 2, x_lo: 2; x = x_hi * 2 + x_lo), y: 8, z: 8, core: 2. Of those that a mesh axis runs over, the one named last changes fastest.
Arguments:
- pairs: bfloat16 [2, 16, 256, 2, 4096], P(None, 'kgrp', None, None, 'ga'), may hold values from -6 to 6
- screening: bfloat16 [16, 2, 4096, 4096], P('kgrp', None, None, 'ga'), may hold values from -0.09375 to 0.09375
- kq_index: int32 [2, 16], replicated, may hold values from 0 to 15, as said below
- umklapp: int32 [2, 16], replicated, may hold values from 0 to 4095
- occupancy: float32 [16, 2], replicated, may hold values from 0.15 to 1.5
Outputs:
- sigma: float32 [16, 2, 256, 256], P('kgrp', None, 'ga')
The draws below stay inside these ranges and needn't reach their ends.
Inputs may be any that keep to these rules, and one draw needn't show every extreme that they name: `kq_index`: each round's row is a permutation of the k-point indices.
All inputs are finite; a program needn't handle non-finite values.
Results may differ from the reference program's by a relative error of at most 0.0029.
Values may be sent and summed in bfloat16 or wider, within the bound.
A program may use at most 64 MiB of HBM per device.

```python
import math
import jax
import jax.numpy as jnp
from jax import lax

NB = 256
NG = 4096
NW = 2
NJ = 2
K_DEV = 1
ROUNDS = 2
NK = 16
N_KGRP = 16


def draw_kq_index(key, part):
    key = jax.random.fold_in(key, 11)
    rows_list = []
    for round_index in range(ROUNDS):
        round_key = jax.random.fold_in(key, round_index)
        rows_list.append(jax.random.permutation(round_key, NK).astype(jnp.int32))
    return jnp.stack(rows_list, axis=0)


def draw_umklapp(key, part):
    key = jax.random.fold_in(key, 23)
    values = jax.random.randint(key, (ROUNDS, NK), 0, NG).astype(jnp.int32)
    values = values.at[0, 0].set(NG - 1)
    values = values.at[ROUNDS - 1, NK - 1].set(0)
    return values


def block_levels(rng, extent, cuts, smallest, top_value):
    def one(axis_at, shards_of):
        steps = jax.random.uniform(jax.random.fold_in(jax.random.fold_in(rng, 6), axis_at), (shards_of,), jnp.float32, smallest / len(cuts), top_value / len(cuts))
        return jnp.repeat(jnp.exp(steps), extent[axis_at] // shards_of).reshape((-1,) + (1,) * (len(extent) - axis_at - 1))

    factor_of = one(*cuts[0])
    for cut in cuts[1:]:
        factor_of = factor_of * one(*cut)
    return factor_of


def gaussian(key, shape, deviation, reach, shards=(), kind=jnp.bfloat16):
    loudness = block_levels(key, shape, shards, -0.22, 0.18) if shards else 1.0
    result = jax.random.normal(key, shape, jnp.float32) * deviation * loudness
    return jnp.minimum(jnp.maximum(result, -reach), reach).astype(kind)


def setup_inputs(seed: int = 0) -> dict:
    key_of = jax.random.split(jax.random.key(seed), 6)
    return {
        "pairs": gaussian(key_of[0], (ROUNDS, NK, NB, NJ, NG), 1.0, 6.0, ((1, 16), (4, 32))),
        "screening": gaussian(key_of[1], (N_KGRP, NW, NG, NG), NG ** -0.5, 0.09375, ((0, 16), (3, 32))),
        "kq_index": draw_kq_index(jax.random.fold_in(key_of[5], 71), 0),
        "umklapp": draw_umklapp(jax.random.fold_in(key_of[5], 71), 0),
        "occupancy": jnp.clip(jnp.exp(jax.random.uniform(key_of[4], (NK, NJ), jnp.float32, math.log(0.15), math.log(1.5))), 0.15, 1.5),
    }


def reference(pairs, screening, kq_index, umklapp, occupancy):
    k_points = jnp.arange(NK, dtype=jnp.int32)

    def one_point(k_point):
        sigma_sum = jnp.zeros((NW, NB, NB), jnp.float32)
        for round_index in range(ROUNDS):
            aligned = jnp.roll(pairs[round_index, k_point], -umklapp[round_index, k_point], axis=2)
            source = (k_point // K_DEV - round_index) % N_KGRP
            screen_block = screening[source].astype(jnp.float32)
            left_rows = aligned.astype(jnp.float32)
            projected = jnp.einsum('bjg,wgh->wbjh', left_rows, screen_block)
            weights = occupancy[kq_index[round_index, k_point]]
            scaled = (projected * weights[None, None, :, None]).astype(jnp.bfloat16)
            scaled = lax.optimization_barrier(scaled).astype(jnp.float32)
            sigma_sum = sigma_sum + jnp.einsum('wbjh,cjh->wbc', scaled, left_rows)
        return sigma_sum / math.sqrt(NG)
    return lax.map(one_point, k_points)
```

```python
import functools
import math

import jax
import jax.numpy as jnp
from jax import lax
from jax.experimental import pallas as pl
from jax.experimental.pallas import tpu as pltpu
from jax.sharding import PartitionSpec as P

ROUNDS = 2
GROUPS = 16
RING = 8
SIDES = 2
CORES = 2
LANES = 128
PARTS = 2
MESH = pl.DeviceIdType.MESH

Z0 = 0
X0 = Z0 + 2 * 4 * PARTS
Y1 = X0 + RING * PARTS
Z1 = Y1 + SIDES * PARTS
C = Z1 + SIDES * 2 * 4 * PARTS
S = C + ROUNDS * SIDES * RING
A = S + ROUNDS * 2
COUNT = A + ROUNDS * RING * SIDES


def kernel(
    pairs,
    screening,
    kq_index,
    umklapp,
    occupancy,
    out,
    all0,
    all1,
    screen,
    shift_rows,
    total,
    right,
    partial,
    sibling_part,
    outgoing,
    incoming,
    send,
    recv,
    local,
):
    group = lax.axis_index("kgrp")
    place = lax.axis_index("ga")
    z = lax.div(place, 4)
    side = lax.rem(lax.div(place, 2), 2)
    core = lax.rem(place, 2)
    tiles = screening.shape[1]
    grid_count = tiles * LANES
    rows = pairs.shape[1]
    piece = rows // PARTS
    gathered = (all0, all1)

    def at(z_at, side_at, core_at):
        return z_at * 4 + side_at * 2 + core_at

    def along(steps):
        return lax.rem(z + steps + 2 * RING, RING)

    before = lax.rem(group + GROUPS - 1, GROUPS)
    after = lax.rem(group + 1, GROUPS)
    upward = (group, at(along(1), side, core))
    downward = (group, at(along(-1), side, core))
    across = (group, at(z, 1 - side, core))
    sibling = (group, at(z, side, 1 - core))

    def copy(source, target, index, device):
        return pltpu.make_async_remote_copy(
            src_ref=source,
            dst_ref=target,
            send_sem=send.at[index],
            recv_sem=recv.at[index],
            device_id=device,
            device_id_type=MESH,
        )

    def cut(part):
        return pl.ds(part * piece, piece)

    def z_of(k):
        steps = lax.div(k + 1, 2)
        return along(jnp.where(lax.rem(k, 2) == 1, -steps, steps))

    def k_of(step, way):
        return 2 * step - 1 + way if step < 4 else 7

    def origin(step, way):
        return along(-step if way == 0 else step)

    def ring_copy(rnd, cross, way, step, part):
        came_from = origin(step - 1, way)
        place_of = at(came_from, lax.rem(side + cross, 2), core)
        target = gathered[rnd].at[place_of, cut(part)]
        source = pairs.at[0, cut(part)] if rnd == 0 and step == 1 else target
        index = (Z0 if rnd == 0 else Z1) + ((cross * 2 + way) * 4 + step - 1) * PARTS + part
        return copy(source, target, index, upward if way == 0 else downward)

    def ring_arrival(rnd, cross, way, step, part):
        place_of = at(origin(step, way), lax.rem(side + cross, 2), core)
        target = gathered[rnd].at[place_of, cut(part)]
        index = (Z0 if rnd == 0 else Z1) + ((cross * 2 + way) * 4 + step - 1) * PARTS + part
        return copy(target, target, index, upward)

    def cross_copy(k, part, own=False):
        target = all0.at[at(z_of(k), side, core), cut(part)]
        source = pairs.at[0, cut(part)] if own else target
        return copy(source, target, X0 + k * PARTS + part, across)

    def cross_arrival(k, part):
        target = all0.at[at(z_of(k), 1 - side, core), cut(part)]
        return copy(target, target, X0 + k * PARTS + part, across)

    def group_copy(cross, part):
        target = all1.at[place, cut(part)]
        device = (before, at(z, lax.rem(side + cross, 2), core))
        return copy(pairs.at[1, cut(part)], target, Y1 + cross * PARTS + part, device)

    def group_arrival(cross, part):
        target = all1.at[at(z, lax.rem(side + cross, 2), core), cut(part)]
        return copy(target, target, Y1 + cross * PARTS + part, sibling)

    def core_copy(rnd, cross, k, own=False):
        target = gathered[rnd].at[at(z_of(k), lax.rem(side + cross, 2), core)]
        source = pairs.at[0] if own else target
        return copy(source, target, C + (rnd * 2 + cross) * RING + k, sibling)

    def core_arrival(rnd, cross, k):
        target = gathered[rnd].at[at(z_of(k), lax.rem(side + cross, 2), 1 - core)]
        return copy(target, target, C + (rnd * 2 + cross) * RING + k, sibling)

    def sum_copy(rnd, w):
        return copy(partial.at[rnd, w, :, 1 - core], sibling_part.at[rnd, w], S + rnd * 2 + w, sibling)

    def spread_copy(rnd, i):
        z_to = lax.rem(z + lax.div(i, 2), RING)
        side_to = lax.rem(side + lax.rem(i, 2), 2)
        device = (group if rnd == 0 else after, at(z_to, side_to, core))
        index = A + rnd * RING * SIDES + i
        return copy(outgoing.at[rnd, z_to * 2 + side_to], incoming.at[rnd, i], index, device)

    barrier = pltpu.get_barrier_semaphore()
    for device in (
        upward,
        downward,
        across,
        sibling,
        (after, place),
        (after, at(z, 1 - side, core)),
    ):
        pl.semaphore_signal(barrier, inc=1, device_id=device, device_id_type=MESH)
    whole = pltpu.make_async_copy(screening, screen.at[:, pl.ds(0, tiles)], local.at[0])
    whole.start()
    wrap = pltpu.make_async_copy(screening.at[:, pl.ds(0, 2)], screen.at[:, pl.ds(tiles, 2)], local.at[1])
    wrap.start()
    mine = pltpu.make_async_copy(pairs.at[0], all0.at[place], local.at[2])
    mine.start()
    pl.semaphore_wait(barrier, 6)

    for part in range(PARTS):
        ring_copy(0, 0, 0, 1, part).start()
        ring_copy(0, 0, 1, 1, part).start()
        cross_copy(0, part, own=True).start()
    for part in range(PARTS):
        for cross in range(SIDES):
            group_copy(cross, part).start()
    core_copy(0, 0, 0, own=True).start()

    k_point = (group, after)
    shift = [umklapp[rnd, k_point[rnd]] for rnd in range(ROUNDS)]
    total[...] = jnp.zeros_like(total)
    for rnd in range(ROUNDS):
        column = lax.broadcasted_iota(jnp.int32, (2 * LANES, 3 * LANES), 1)
        row = lax.broadcasted_iota(jnp.int32, (2 * LANES, 3 * LANES), 0)
        hit = column == row + lax.rem(grid_count - shift[rnd], LANES)
        shift_rows[rnd] = jnp.where(hit, 1.0, 0.0).astype(jnp.bfloat16)
    whole.wait()
    wrap.wait()
    mine.wait()

    def multiply(rnd, cross, first, last):
        def one(k, carry):
            core_arrival(rnd, cross, k).wait_recv()
            chip = z_of(k) * 2 + lax.rem(side + cross, 2)
            start = lax.rem(chip * 2 * LANES + grid_count - shift[rnd], grid_count)
            tile = lax.div(start, LANES)
            met = jnp.concatenate(
                [jnp.concatenate([screen[w, tile + i] for i in range(3)], axis=0) for w in range(2)], axis=1
            )
            met = jnp.dot(shift_rows[rnd], met, preferred_element_type=jnp.float32)
            left = jnp.concatenate([gathered[rnd][chip * 2], gathered[rnd][chip * 2 + 1]], axis=1)
            product = jnp.dot(left, met.astype(jnp.bfloat16), preferred_element_type=jnp.float32)
            for w in range(2):
                total[rnd, w] += product[:, w * LANES : (w + 1) * LANES]
            return carry

        lax.fori_loop(first, last, one, 0)

    def take_across(first, last):
        for k in range(first, last):
            for part in range(PARTS):
                cross_arrival(k, part).wait_recv()
            core_copy(0, 1, k).start()

    def contract(rnd):
        begin = lax.rem(place + lax.div(shift[rnd], LANES), 2 * RING * SIDES)
        follow = lax.rem(begin + 1, 2 * RING * SIDES)
        row = lax.broadcasted_iota(jnp.int32, (2 * LANES, LANES), 0)
        column = lax.broadcasted_iota(jnp.int32, (2 * LANES, LANES), 1)
        hit = row == column + lax.rem(shift[rnd], LANES)
        pick = jnp.where(hit, 1.0, 0.0).astype(jnp.bfloat16)
        near = jnp.concatenate([gathered[rnd][begin], gathered[rnd][follow]], axis=1)
        right[...] = jnp.dot(near, pick, preferred_element_type=jnp.float32)
        bands = rows // 2
        others = jnp.concatenate(
            [right[pl.ds(j, bands, stride=2), :].astype(jnp.bfloat16) for j in range(2)], axis=1
        )
        weight = [occupancy[kq_index[rnd, k_point[rnd]], j] for j in range(2)]
        for w in range(2):
            scaled = [total[rnd, w, pl.ds(j, bands, stride=2), :] * weight[j] for j in range(2)]
            left = jnp.concatenate(scaled, axis=1).astype(jnp.bfloat16)
            sums = lax.dot_general(
                left, others, (((1,), (1,)), ((), ())), preferred_element_type=jnp.float32
            )
            partial[rnd, w] = sums.reshape(partial.shape[2:])
            sum_copy(rnd, w).start()

    def spread(rnd):
        added = []
        for w in range(2):
            sum_copy(rnd, w).wait_recv()
            added.append(partial[rnd, w, :, core] + sibling_part[rnd, w])
        outgoing[rnd] = jnp.concatenate(added, axis=1).astype(jnp.bfloat16)

        def one(i, carry):
            spread_copy(rnd, i).start()
            return carry

        lax.fori_loop(1 - rnd, RING * SIDES, one, 0)

    for step in range(1, 4):
        for part in range(PARTS):
            for way in range(2):
                ring_arrival(0, 0, way, step, part).wait_recv()
                if step < 3 or part * 2 // PARTS == way:
                    ring_copy(0, 0, way, step + 1, part).start()
                cross_copy(k_of(step, way), part).start()
        for way in range(2):
            core_copy(0, 0, k_of(step, way)).start()
        multiply(0, 0, max(0, 2 * step - 3), 2 * step - 1)

    for cross in range(SIDES):
        for part in range(PARTS):
            group_arrival(cross, part).wait_recv()
            for way in range(2):
                ring_copy(1, cross, way, 1, part).start()
        core_copy(1, cross, 0).start()
    for part in range(PARTS):
        ring_arrival(0, 0, part * 2 // PARTS, 4, part).wait_recv()
        cross_copy(7, part).start()
    core_copy(0, 0, 7).start()
    multiply(0, 0, 5, 7)

    between = {
        (1, 0): lambda: (take_across(0, 3), multiply(0, 0, 7, 8)),
        (1, 1): lambda: (take_across(3, 4), multiply(0, 1, 0, 2)),
        (1, 2): lambda: multiply(0, 1, 2, 4),
        (1, 3): lambda: (take_across(4, 5), multiply(1, 0, 0, 1)),
        (2, 0): lambda: (take_across(5, 6), multiply(0, 1, 4, 5), multiply(1, 1, 0, 1)),
        (2, 1): lambda: multiply(1, 0, 1, 3),
        (2, 2): lambda: (take_across(6, 7), multiply(1, 1, 1, 3)),
        (2, 3): lambda: multiply(0, 1, 5, 6),
        (3, 0): lambda: multiply(0, 1, 6, 7),
        (3, 1): lambda: multiply(1, 0, 3, 5),
        (3, 2): lambda: (take_across(7, 8), multiply(1, 1, 3, 5)),
        (3, 3): lambda: (multiply(0, 1, 7, 8), contract(0)),
        (4, 0): lambda: (spread(0), multiply(1, 0, 5, 7)),
        (4, 1): lambda: multiply(1, 1, 5, 7),
    }
    for step in range(1, 5):
        for cross in range(SIDES):
            for part in range(PARTS):
                for way in range(2):
                    if step == 4 and part * 2 // PARTS != way:
                        continue
                    ring_arrival(1, cross, way, step, part).wait_recv()
                    if step < 3 or (step == 3 and part * 2 // PARTS == way):
                        ring_copy(1, cross, way, step + 1, part).start()
                if step < 4:
                    if part == PARTS - 1:
                        for way in range(2):
                            core_copy(1, cross, k_of(step, way)).start()
                    between[(step, cross * 2 + part * 2 // PARTS)]()
            if step == 4:
                core_copy(1, cross, 7).start()
                between[(step, cross)]()
    multiply(1, 0, 7, 8)
    multiply(1, 1, 7, 8)
    contract(1)
    spread(1)

    def settle(i, carry):
        spread_copy(0, i).wait_recv()
        return carry

    lax.fori_loop(1, RING * SIDES, settle, 0)
    chip = z * 2 + side
    own = jnp.concatenate([partial[0, w, chip, core] + sibling_part[0, w, chip] for w in range(2)], axis=0)
    result = own + jnp.sum(incoming[0, 1:].astype(jnp.float32), axis=0)
    for step in range(1, 5):
        for part in range(PARTS):
            for way in range(2):
                if step == 4 and part * 2 // PARTS != way:
                    continue
                ring_copy(0, 0, way, step, part).wait_send()
                for cross in range(SIDES):
                    ring_copy(1, cross, way, step, part).wait_send()
    for part in range(PARTS):
        for cross in range(SIDES):
            group_copy(cross, part).wait_send()
        for k in range(RING):
            cross_copy(k, part, own=k == 0).wait_send()
    for rnd in range(ROUNDS):
        for cross in range(SIDES):
            for k in range(RING):
                core_copy(rnd, cross, k).wait_send()
        for w in range(2):
            sum_copy(rnd, w).wait_send()

    def sent(i, carry):
        spread_copy(0, i).wait_send()
        return carry

    lax.fori_loop(1, RING * SIDES, sent, 0)

    def last(i, carry):
        spread_copy(1, i).wait()
        return carry

    lax.fori_loop(0, RING * SIDES, last, 0)
    result = result + jnp.sum(incoming[1].astype(jnp.float32), axis=0)
    bands = out.shape[1]
    for w in range(2):
        out[w] = result[w * bands : (w + 1) * bands] * (1.0 / math.sqrt(grid_count))


def per_device(pairs, screening, kq_index, umklapp, occupancy):
    rounds, k_count, band_count, summed_count, column_count = pairs.shape
    rows = band_count * summed_count
    grid_count = screening.shape[2]
    devices = grid_count // column_count
    bands = band_count // devices
    chips = RING * SIDES
    sigma = pl.pallas_call(
        kernel,
        out_shape=jax.ShapeDtypeStruct((2, bands, band_count), jnp.float32),
        in_specs=[
            pl.BlockSpec(memory_space=pl.ANY),
            pl.BlockSpec(memory_space=pl.ANY),
            pl.BlockSpec(memory_space=pltpu.SMEM),
            pl.BlockSpec(memory_space=pltpu.SMEM),
            pl.BlockSpec(memory_space=pltpu.SMEM),
        ],
        out_specs=pl.BlockSpec(memory_space=pltpu.VMEM),
        scratch_shapes=[
            pltpu.VMEM((devices, rows, column_count), jnp.bfloat16),
            pltpu.VMEM((devices, rows, column_count), jnp.bfloat16),
            pltpu.VMEM((2, devices + 2, LANES, column_count), jnp.bfloat16),
            pltpu.VMEM((ROUNDS, 2 * LANES, 3 * LANES), jnp.bfloat16),
            pltpu.VMEM((ROUNDS, 2, rows, column_count), jnp.float32),
            pltpu.VMEM((rows, column_count), jnp.float32),
            pltpu.VMEM((ROUNDS, 2, chips, 2, bands, band_count), jnp.float32),
            pltpu.VMEM((ROUNDS, 2, chips, bands, band_count), jnp.float32),
            pltpu.VMEM((ROUNDS, chips, 2 * bands, band_count), jnp.bfloat16),
            pltpu.VMEM((ROUNDS, chips, 2 * bands, band_count), jnp.bfloat16),
            pltpu.SemaphoreType.DMA((COUNT,)),
            pltpu.SemaphoreType.DMA((COUNT,)),
            pltpu.SemaphoreType.DMA((3,)),
        ],
        compiler_params=pltpu.CompilerParams(
            collective_id=0, has_side_effects=True, vmem_limit_bytes=40 << 20
        ),
    )(
        pairs.reshape(rounds, rows, column_count),
        screening.reshape(2, devices, LANES, column_count),
        kq_index,
        umklapp,
        occupancy,
    )
    return sigma[None]


def solution(mesh):
    return jax.shard_map(
        per_device,
        mesh=mesh,
        in_specs=(P(None, "kgrp", None, None, "ga"), P("kgrp", None, None, "ga"), P(), P(), P()),
        out_specs=P("kgrp", None, "ga", None),
        check_vma=False,
    )
```

```python
import functools
import math

import jax
import jax.numpy as jnp
from jax import lax
from jax.experimental import pallas as pl
from jax.experimental.pallas import tpu as pltpu
from jax.sharding import PartitionSpec as P

ROUNDS = 2
GROUPS = 16
RING = 8
SIDES = 2
CORES = 2
LANES = 128
PARTS = 2
MESH = pl.DeviceIdType.MESH

Z0 = 0
X0 = Z0 + 2 * 4 * PARTS
X1 = X0 + RING * PARTS
Y1 = X1 + PARTS
Z1 = Y1 + SIDES * PARTS
C = Z1 + SIDES * 2 * 4 * PARTS
S = C + ROUNDS * SIDES * RING * PARTS
A = S + ROUNDS * 2
COUNT = A + ROUNDS * RING * SIDES


def kernel(
    pairs,
    screening,
    kq_index_all,
    umklapp_all,
    occupancy_all,
    out,
    all0,
    all1,
    screen,
    shift_rows,
    total,
    right,
    partial,
    sibling_part,
    outgoing,
    incoming,
    last_rows,
    kq_index,
    umklapp,
    occupancy,
    send,
    recv,
    local,
):
    group = lax.axis_index("kgrp")
    place = lax.axis_index("ga")
    z = lax.div(place, 4)
    side = lax.rem(lax.div(place, 2), 2)
    core = lax.rem(place, 2)
    tiles = screening.shape[1]
    grid_count = tiles * LANES
    rows = pairs.shape[1]
    piece = rows // PARTS
    gathered = (all0, all1)

    def at(z_at, side_at, core_at):
        return z_at * 4 + side_at * 2 + core_at

    def along(steps):
        return lax.rem(z + steps + 2 * RING, RING)

    before = lax.rem(group + GROUPS - 1, GROUPS)
    after = lax.rem(group + 1, GROUPS)
    upward = (group, at(along(1), side, core))
    downward = (group, at(along(-1), side, core))
    across = (group, at(z, 1 - side, core))
    sibling = (group, at(z, side, 1 - core))

    def copy(source, target, index, device):
        return pltpu.make_async_remote_copy(
            src_ref=source,
            dst_ref=target,
            send_sem=send.at[index],
            recv_sem=recv.at[index],
            device_id=device,
            device_id_type=MESH,
        )

    def cut(part):
        return pl.ds(part * piece, piece)

    def z_of(k):
        steps = lax.div(k + 1, 2)
        return along(jnp.where(lax.rem(k, 2) == 1, -steps, steps))

    def k_of(step, way):
        return 2 * step - 1 + way if step < 4 else 7

    def origin(step, way):
        return along(-step if way == 0 else step)

    def ring_copy(rnd, cross, way, step, part):
        came_from = origin(step - 1, way)
        place_of = at(came_from, lax.rem(side + cross, 2), core)
        target = gathered[rnd].at[place_of, cut(part)]
        source = pairs.at[0, cut(part)] if rnd == 0 and step == 1 else target
        index = (Z0 if rnd == 0 else Z1) + ((cross * 2 + way) * 4 + step - 1) * PARTS + part
        return copy(source, target, index, upward if way == 0 else downward)

    def ring_arrival(rnd, cross, way, step, part):
        place_of = at(origin(step, way), lax.rem(side + cross, 2), core)
        target = gathered[rnd].at[place_of, cut(part)]
        index = (Z0 if rnd == 0 else Z1) + ((cross * 2 + way) * 4 + step - 1) * PARTS + part
        return copy(target, target, index, upward)

    def cross_copy(rnd, k, part, own=False):
        target = gathered[rnd].at[at(z_of(k), side, core), cut(part)]
        source = pairs.at[0, cut(part)] if own else target
        return copy(source, target, (X0 + k * PARTS if rnd == 0 else X1) + part, across)

    def cross_arrival(rnd, k, part):
        target = gathered[rnd].at[at(z_of(k), 1 - side, core), cut(part)]
        return copy(target, target, (X0 + k * PARTS if rnd == 0 else X1) + part, across)

    def group_copy(cross, part):
        target = all1.at[place, cut(part)]
        device = (before, at(z, lax.rem(side + cross, 2), core))
        return copy(pairs.at[1, cut(part)], target, Y1 + cross * PARTS + part, device)

    def group_arrival(cross, part):
        target = all1.at[at(z, lax.rem(side + cross, 2), core), cut(part)]
        return copy(target, target, Y1 + cross * PARTS + part, sibling)

    def core_copy(rnd, cross, k, part, own=False):
        target = gathered[rnd].at[at(z_of(k), lax.rem(side + cross, 2), core), cut(part)]
        source = pairs.at[0, cut(part)] if own else target
        return copy(source, target, C + ((rnd * 2 + cross) * RING + k) * PARTS + part, sibling)

    def core_arrival(rnd, cross, k, part):
        target = gathered[rnd].at[at(z_of(k), lax.rem(side + cross, 2), 1 - core), cut(part)]
        return copy(target, target, C + ((rnd * 2 + cross) * RING + k) * PARTS + part, sibling)

    def sum_copy(rnd, w):
        return copy(partial.at[rnd, w, :, 1 - core], sibling_part.at[rnd, w], S + rnd * 2 + w, sibling)

    def spread_copy(rnd, i):
        z_to = lax.rem(z + lax.div(i, 2), RING)
        side_to = lax.rem(side + lax.rem(i, 2), 2)
        device = (group if rnd == 0 else after, at(z_to, side_to, core))
        index = A + rnd * RING * SIDES + i
        return copy(outgoing.at[rnd, z_to * 2 + side_to], incoming.at[rnd, i], index, device)

    barrier = pltpu.get_barrier_semaphore()
    for device in (
        upward,
        downward,
        across,
        sibling,
        (after, place),
        (after, at(z, 1 - side, core)),
    ):
        pl.semaphore_signal(barrier, inc=1, device_id=device, device_id_type=MESH)
    whole = pltpu.make_async_copy(screening, screen.at[:, pl.ds(0, tiles)], local.at[0])
    whole.start()
    wrap = pltpu.make_async_copy(screening.at[:, pl.ds(0, 2)], screen.at[:, pl.ds(tiles, 2)], local.at[1])
    wrap.start()
    mine = pltpu.make_async_copy(pairs.at[0], all0.at[place], local.at[2])
    mine.start()
    tables = [
        pltpu.make_async_copy(source, target, local.at[3 + i])
        for i, (source, target) in enumerate(
            ((kq_index_all, kq_index), (umklapp_all, umklapp), (occupancy_all, occupancy))
        )
    ]
    for table in tables:
        table.start()
    pl.semaphore_wait(barrier, 6)

    for part in range(PARTS):
        ring_copy(0, 0, 0, 1, part).start()
        ring_copy(0, 0, 1, 1, part).start()
        cross_copy(0, 0, part, own=True).start()
        group_copy(0, part).start()
    for part in range(PARTS):
        group_copy(1, part).start()
        core_copy(0, 0, 0, part, own=True).start()
    for table in tables:
        table.wait()

    k_point = (group, after)
    shift = [umklapp[rnd, k_point[rnd]] for rnd in range(ROUNDS)]
    total[...] = jnp.zeros_like(total)
    for rnd in range(ROUNDS):
        column = lax.broadcasted_iota(jnp.int32, (2 * LANES, 3 * LANES), 1)
        row = lax.broadcasted_iota(jnp.int32, (2 * LANES, 3 * LANES), 0)
        hit = column == row + lax.rem(grid_count - shift[rnd], LANES)
        shift_rows[rnd] = jnp.where(hit, 1.0, 0.0).astype(jnp.bfloat16)
    whole.wait()
    wrap.wait()
    mine.wait()

    def met_rows(rnd, cross, k):
        chip = z_of(k) * 2 + lax.rem(side + cross, 2)
        start = lax.rem(chip * 2 * LANES + grid_count - shift[rnd], grid_count)
        tile = lax.div(start, LANES)
        near = jnp.concatenate(
            [jnp.concatenate([screen[w, tile + i] for i in range(3)], axis=0) for w in range(2)], axis=1
        )
        near = jnp.dot(shift_rows[rnd], near, preferred_element_type=jnp.float32)
        return near.astype(jnp.bfloat16)

    def multiply(rnd, *blocks, met=None):
        left = []
        for cross, k in blocks:
            for part in range(PARTS):
                core_arrival(rnd, cross, k, part).wait_recv()
            chip = z_of(k) * 2 + lax.rem(side + cross, 2)
            left += [gathered[rnd][chip * 2], gathered[rnd][chip * 2 + 1]]
        if met is None:
            met = jnp.concatenate([met_rows(rnd, cross, k) for cross, k in blocks], axis=0)
        product = jnp.dot(jnp.concatenate(left, axis=1), met, preferred_element_type=jnp.float32)
        for w in range(2):
            total[rnd, w] += product[:, w * LANES : (w + 1) * LANES]

    def take_across(rnd, k):
        for part in range(PARTS):
            cross_arrival(rnd, k, part).wait_recv()
            core_copy(rnd, 1, k, part).start()

    def take_group(cross):
        for part in range(PARTS):
            group_arrival(cross, part).wait_recv()
            for way in range(2):
                ring_copy(1, cross, way, 1, part).start()
            core_copy(1, cross, 0, part).start()

    def last_step(rnd, cross):
        return 3 if rnd == 1 and cross == 1 else 4

    def ways(step, part):
        return (part,) if step == 4 else (0, 1)

    def take_ring(rnd, cross, step):
        for part in range(PARTS):
            for way in ways(step, part):
                ring_arrival(rnd, cross, way, step, part).wait_recv()
                if step < last_step(rnd, cross) and way in ways(step + 1, part):
                    ring_copy(rnd, cross, way, step + 1, part).start()
                k = k_of(step, way)
                if rnd == 0 or (cross == 0 and step == 4):
                    cross_copy(rnd, k, part).start()
                core_copy(rnd, cross, k, part).start()

    def contract(rnd):
        begin = lax.rem(place + lax.div(shift[rnd], LANES), 2 * RING * SIDES)
        follow = lax.rem(begin + 1, 2 * RING * SIDES)
        row = lax.broadcasted_iota(jnp.int32, (2 * LANES, LANES), 0)
        column = lax.broadcasted_iota(jnp.int32, (2 * LANES, LANES), 1)
        hit = row == column + lax.rem(shift[rnd], LANES)
        pick = jnp.where(hit, 1.0, 0.0).astype(jnp.bfloat16)
        near = jnp.concatenate([gathered[rnd][begin], gathered[rnd][follow]], axis=1)
        right[...] = jnp.dot(near, pick, preferred_element_type=jnp.float32)
        bands = rows // 2
        others = jnp.concatenate(
            [right[pl.ds(j, bands, stride=2), :].astype(jnp.bfloat16) for j in range(2)], axis=1
        )
        weight = [occupancy[j, kq_index[rnd, k_point[rnd]]] for j in range(2)]
        for w in range(2):
            scaled = [total[rnd, w, pl.ds(j, bands, stride=2), :] * weight[j] for j in range(2)]
            left = jnp.concatenate(scaled, axis=1).astype(jnp.bfloat16)
            sums = lax.dot_general(
                left, others, (((1,), (1,)), ((), ())), preferred_element_type=jnp.float32
            )
            partial[rnd, w] = sums.reshape(partial.shape[2:])
            sum_copy(rnd, w).start()

    def spread(rnd):
        added = []
        for w in range(2):
            sum_copy(rnd, w).wait_recv()
            added.append(partial[rnd, w, :, core] + sibling_part[rnd, w])
        outgoing[rnd] = jnp.concatenate(added, axis=1).astype(jnp.bfloat16)

        def one(i, carry):
            spread_copy(rnd, i).start()
            return carry

        lax.fori_loop(1 - rnd, RING * SIDES, one, 0)

    take_ring(0, 0, 1)
    take_group(0)
    multiply(0, (0, 0), (0, 1), (0, 2))
    take_ring(0, 0, 2)
    take_group(1)
    take_across(0, 0)
    multiply(0, (0, 3), (0, 4), (1, 0))
    take_ring(1, 0, 1)
    multiply(1, (0, 0), (1, 0), (0, 1), (0, 2))
    take_ring(0, 0, 3)
    take_across(0, 1)
    multiply(0, (0, 5), (0, 6), (1, 1))
    take_ring(1, 0, 2)
    take_across(0, 2)
    multiply(1, (0, 3), (0, 4))
    take_ring(1, 1, 1)
    take_across(0, 3)
    multiply(0, (1, 2), (1, 3))
    multiply(1, (1, 1), (1, 2))
    take_ring(1, 0, 3)
    take_across(0, 4)
    multiply(1, (0, 5), (0, 6))
    take_ring(0, 0, 4)
    take_ring(1, 0, 4)
    take_across(0, 5)
    multiply(0, (0, 7), (1, 4), (1, 5))
    take_ring(1, 1, 2)
    take_across(0, 6)
    multiply(1, (0, 7), (1, 3), (1, 4))
    for i, k in enumerate((5, 6, 7)):
        last_rows[i] = met_rows(1, 1, k)
    take_across(0, 7)
    multiply(0, (1, 6), (1, 7))
    contract(0)
    take_ring(1, 1, 3)
    spread(0)
    take_across(1, 7)
    multiply(1, (1, 5), (1, 6), (1, 7), met=jnp.concatenate([last_rows[i] for i in range(3)], axis=0))
    contract(1)
    spread(1)

    def settle(i, carry):
        spread_copy(0, i).wait_recv()
        return carry

    lax.fori_loop(1, RING * SIDES, settle, 0)
    chip = z * 2 + side
    own = jnp.concatenate([partial[0, w, chip, core] + sibling_part[0, w, chip] for w in range(2)], axis=0)
    result = own + jnp.sum(incoming[0, 1:].astype(jnp.float32), axis=0)
    for rnd, cross in ((0, 0), (1, 0), (1, 1)):
        for step in range(1, last_step(rnd, cross) + 1):
            for part in range(PARTS):
                for way in ways(step, part):
                    ring_copy(rnd, cross, way, step, part).wait_send()
    for part in range(PARTS):
        for cross in range(SIDES):
            group_copy(cross, part).wait_send()
        for k in range(RING):
            cross_copy(0, k, part, own=k == 0).wait_send()
        cross_copy(1, 7, part).wait_send()
    for rnd in range(ROUNDS):
        for cross in range(SIDES):
            for k in range(RING):
                for part in range(PARTS):
                    core_copy(rnd, cross, k, part).wait_send()
        for w in range(2):
            sum_copy(rnd, w).wait_send()

    def sent(i, carry):
        spread_copy(0, i).wait_send()
        return carry

    lax.fori_loop(1, RING * SIDES, sent, 0)

    def last(i, carry):
        spread_copy(1, i).wait()
        return carry

    lax.fori_loop(0, RING * SIDES, last, 0)
    result = result + jnp.sum(incoming[1].astype(jnp.float32), axis=0)
    bands = out.shape[1]
    for w in range(2):
        out[w] = result[w * bands : (w + 1) * bands] * (1.0 / math.sqrt(grid_count))


def per_device(pairs, screening, kq_index, umklapp, occupancy):
    rounds, k_count, band_count, summed_count, column_count = pairs.shape
    rows = band_count * summed_count
    grid_count = screening.shape[2]
    devices = grid_count // column_count
    bands = band_count // devices
    chips = RING * SIDES
    sigma = pl.pallas_call(
        kernel,
        out_shape=jax.ShapeDtypeStruct((2, bands, band_count), jnp.float32),
        in_specs=[
            pl.BlockSpec(memory_space=pl.ANY),
            pl.BlockSpec(memory_space=pl.ANY),
            pl.BlockSpec(memory_space=pl.ANY),
            pl.BlockSpec(memory_space=pl.ANY),
            pl.BlockSpec(memory_space=pl.ANY),
        ],
        out_specs=pl.BlockSpec(memory_space=pltpu.VMEM),
        scratch_shapes=[
            pltpu.VMEM((devices, rows, column_count), jnp.bfloat16),
            pltpu.VMEM((devices, rows, column_count), jnp.bfloat16),
            pltpu.VMEM((2, devices + 2, LANES, column_count), jnp.bfloat16),
            pltpu.VMEM((ROUNDS, 2 * LANES, 3 * LANES), jnp.bfloat16),
            pltpu.VMEM((ROUNDS, 2, rows, column_count), jnp.float32),
            pltpu.VMEM((rows, column_count), jnp.float32),
            pltpu.VMEM((ROUNDS, 2, chips, 2, bands, band_count), jnp.float32),
            pltpu.VMEM((ROUNDS, 2, chips, bands, band_count), jnp.float32),
            pltpu.VMEM((ROUNDS, chips, 2 * bands, band_count), jnp.bfloat16),
            pltpu.VMEM((ROUNDS, chips, 2 * bands, band_count), jnp.bfloat16),
            pltpu.VMEM((3, 2 * LANES, 2 * column_count), jnp.bfloat16),
            pltpu.SMEM(kq_index.shape, jnp.int32),
            pltpu.SMEM(umklapp.shape, jnp.int32),
            pltpu.SMEM(occupancy.shape[::-1], jnp.float32),
            pltpu.SemaphoreType.DMA((COUNT,)),
            pltpu.SemaphoreType.DMA((COUNT,)),
            pltpu.SemaphoreType.DMA((6,)),
        ],
        compiler_params=pltpu.CompilerParams(
            collective_id=0, has_side_effects=True, vmem_limit_bytes=62 << 20
        ),
    )(
        pairs.reshape(rounds, rows, column_count),
        screening.reshape(2, devices, LANES, column_count),
        kq_index,
        umklapp,
        occupancy.T,
    )
    return sigma[None]


def solution(mesh):
    return jax.shard_map(
        per_device,
        mesh=mesh,
        in_specs=(P(None, "kgrp", None, None, "ga"), P("kgrp", None, None, "ga"), P(), P(), P()),
        out_specs=P("kgrp", None, "ga", None),
        check_vma=False,
    )
```

```python
import functools
import math

import jax
import jax.numpy as jnp
from jax import lax
from jax.experimental import pallas as pl
from jax.experimental.pallas import tpu as pltpu
from jax.sharding import PartitionSpec as P

ROUNDS = 2
GROUPS = 16
RING = 8
SIDES = 2
CORES = 2
LANES = 128
PARTS = 2
MESH = pl.DeviceIdType.MESH

Z0 = 0
X0 = Z0 + 2 * 4 * PARTS
X1 = X0 + RING * PARTS
Y1 = X1 + 2 * PARTS
Z1 = Y1 + PARTS
C = Z1 + SIDES * 2 * 4 * PARTS
R = C + 2
S = R + ROUNDS
A = S + ROUNDS * 2
COUNT = A + ROUNDS * RING * SIDES


def kernel(
    pairs,
    screening,
    kq_index_all,
    umklapp_all,
    occupancy_all,
    out,
    all0,
    all1,
    screen,
    shift_rows,
    total,
    right,
    right_mine,
    right_theirs,
    partial,
    sibling_part,
    outgoing,
    incoming,
    last_rows,
    kq_index,
    umklapp,
    occupancy,
    send,
    recv,
    local,
):
    group = lax.axis_index("kgrp")
    place = lax.axis_index("ga")
    z = lax.div(place, 4)
    side = lax.rem(lax.div(place, 2), 2)
    core = lax.rem(place, 2)
    tiles = screening.shape[1]
    grid_count = tiles * LANES
    rows = pairs.shape[1]
    piece = rows // PARTS
    gathered = (all0, all1)

    def at(z_at, side_at, core_at):
        return z_at * 4 + side_at * 2 + core_at

    def chip_at(z_at, side_at):
        return z_at * 2 + side_at

    def along(steps):
        return lax.rem(z + steps + 2 * RING, RING)

    before = lax.rem(group + GROUPS - 1, GROUPS)
    after = lax.rem(group + 1, GROUPS)
    upward = (group, at(along(1), side, core))
    downward = (group, at(along(-1), side, core))
    across = (group, at(z, 1 - side, core))
    sibling = (group, at(z, side, 1 - core))

    def copy(source, target, index, device):
        return pltpu.make_async_remote_copy(
            src_ref=source,
            dst_ref=target,
            send_sem=send.at[index],
            recv_sem=recv.at[index],
            device_id=device,
            device_id_type=MESH,
        )

    def cut(part):
        return pl.ds(part * piece, piece)

    def z_of(k):
        steps = lax.div(k + 1, 2)
        return along(jnp.where(lax.rem(k, 2) == 1, -steps, steps))

    def k_of(step, way):
        return 2 * step - 1 + way if step < 4 else 7

    def origin(step, way):
        return along(-step if way == 0 else step)

    def ring_copy(rnd, cross, way, step, part):
        came_from = origin(step - 1, way)
        place_of = chip_at(came_from, lax.rem(side + cross, 2))
        target = gathered[rnd].at[place_of, cut(part)]
        source = pairs.at[0, cut(part)] if rnd == 0 and step == 1 else target
        index = (Z0 if rnd == 0 else Z1) + ((cross * 2 + way) * 4 + step - 1) * PARTS + part
        return copy(source, target, index, upward if way == 0 else downward)

    def ring_arrival(rnd, cross, way, step, part):
        place_of = chip_at(origin(step, way), lax.rem(side + cross, 2))
        target = gathered[rnd].at[place_of, cut(part)]
        index = (Z0 if rnd == 0 else Z1) + ((cross * 2 + way) * 4 + step - 1) * PARTS + part
        return copy(target, target, index, upward)

    def cross_copy(rnd, k, part, own=False):
        target = gathered[rnd].at[chip_at(z_of(k), side), cut(part)]
        source = pairs.at[0, cut(part)] if own else target
        return copy(source, target, (X0 + k * PARTS if rnd == 0 else X1 + (k // 7) * PARTS) + part, across)

    def cross_arrival(rnd, k, part):
        target = gathered[rnd].at[chip_at(z_of(k), 1 - side), cut(part)]
        return copy(target, target, (X0 + k * PARTS if rnd == 0 else X1 + (k // 7) * PARTS) + part, across)

    def group_copy(part):
        target = all1.at[chip_at(z, side), cut(part)]
        return copy(pairs.at[1, cut(part)], target, Y1 + part, (before, place))

    def group_arrival(part):
        target = all1.at[chip_at(z, side), cut(part)]
        return copy(target, target, Y1 + part, sibling)

    def screen_copy(wrap):
        first, count = (tiles, 1) if wrap else (0, tiles)
        target = screen.at[core, :, pl.ds(first, count)]
        return copy(screening.at[:, pl.ds(0, count)], target, C + wrap, sibling)

    def screen_arrival(wrap):
        first, count = (tiles, 1) if wrap else (0, tiles)
        target = screen.at[1 - core, :, pl.ds(first, count)]
        return copy(target, target, C + wrap, sibling)

    def right_copy(rnd):
        return copy(right_mine.at[rnd], right_theirs.at[rnd], R + rnd, sibling)

    def sum_copy(rnd, w):
        return copy(partial.at[rnd, w, :, 1 - core], sibling_part.at[rnd, w], S + rnd * 2 + w, sibling)

    def spread_copy(rnd, i):
        turn = lax.div(i, 2)
        steps = jnp.where(lax.rem(turn, 2) == 1, 4 - lax.div(turn + 1, 2), 4 + lax.div(turn, 2))
        z_to = along(steps)
        side_to = lax.rem(side + 1 - lax.rem(i, 2), 2)
        device = (group if rnd == 0 else after, at(z_to, side_to, core))
        index = A + rnd * RING * SIDES + i
        return copy(outgoing.at[rnd, z_to * 2 + side_to], incoming.at[rnd, i], index, device)

    barrier = pltpu.get_barrier_semaphore()
    for device in (
        upward,
        downward,
        across,
        sibling,
        (after, place),
        (before, place),
    ):
        pl.semaphore_signal(barrier, inc=1, device_id=device, device_id_type=MESH)
    whole = pltpu.make_async_copy(screening, screen.at[core, :, pl.ds(0, tiles)], local.at[0])
    whole.start()
    wrap = pltpu.make_async_copy(screening.at[:, pl.ds(0, 1)], screen.at[core, :, pl.ds(tiles, 1)], local.at[1])
    wrap.start()
    mine = pltpu.make_async_copy(pairs.at[0], all0.at[chip_at(z, side)], local.at[2])
    mine.start()
    tables = [
        pltpu.make_async_copy(source, target, local.at[3 + i])
        for i, (source, target) in enumerate(
            ((kq_index_all, kq_index), (umklapp_all, umklapp), (occupancy_all, occupancy))
        )
    ]
    for table in tables:
        table.start()
    pl.semaphore_wait(barrier, 6)

    for part in range(PARTS):
        ring_copy(0, 0, 0, 1, part).start()
        ring_copy(0, 0, 1, 1, part).start()
        cross_copy(0, 0, part, own=True).start()
        group_copy(part).start()
    for again in range(2):
        screen_copy(again).start()
    for table in tables:
        table.wait()

    k_point = (group, after)
    shift = [umklapp[rnd, k_point[rnd]] for rnd in range(ROUNDS)]
    total[...] = jnp.zeros_like(total)
    for rnd in range(ROUNDS):
        column = lax.broadcasted_iota(jnp.int32, (LANES, 2 * LANES), 1)
        row = lax.broadcasted_iota(jnp.int32, (LANES, 2 * LANES), 0)
        hit = column == row + lax.rem(grid_count - shift[rnd], LANES)
        shift_rows[rnd] = jnp.where(hit, 1.0, 0.0).astype(jnp.bfloat16)

    def met_rows(rnd, cross, k):
        block = chip_at(z_of(k), lax.rem(side + cross, 2)) * 2 + core
        start = lax.rem(block * LANES + grid_count - shift[rnd], grid_count)
        tile = lax.div(start, LANES)
        near = jnp.concatenate(
            [
                jnp.concatenate([screen[c, w, tile + i] for i in range(2)], axis=0)
                for w in range(2)
                for c in range(CORES)
            ],
            axis=1,
        )
        near = jnp.dot(shift_rows[rnd], near, preferred_element_type=jnp.float32)
        return near.astype(jnp.bfloat16)

    def multiply(rnd, *blocks, met=None):
        left = [gathered[rnd][chip_at(z_of(k), lax.rem(side + cross, 2))] for cross, k in blocks]
        if met is None:
            met = jnp.concatenate([met_rows(rnd, cross, k) for cross, k in blocks], axis=0)
        product = jnp.dot(jnp.concatenate(left, axis=1), met, preferred_element_type=jnp.float32)
        for i in range(2 * CORES):
            total[rnd, i] += product[:, i * LANES : (i + 1) * LANES]

    def take_across(rnd, k):
        for part in range(PARTS):
            cross_arrival(rnd, k, part).wait_recv()

    def take_group():
        for part in range(PARTS):
            group_arrival(part).wait_recv()
            for way in range(2):
                ring_copy(1, 0, way, 1, part).start()
            cross_copy(1, 0, part).start()

    def take_group_across():
        for part in range(PARTS):
            cross_arrival(1, 0, part).wait_recv()
            for way in range(2):
                ring_copy(1, 1, way, 1, part).start()

    def last_step(rnd, cross):
        return 3 if rnd == 1 and cross == 1 else 4

    def ways(step, part):
        return (part,) if step == 4 else (0, 1)

    def take_ring(rnd, cross, step, hand_across=True):
        for part in range(PARTS):
            for way in ways(step, part):
                ring_arrival(rnd, cross, way, step, part).wait_recv()
                if step < last_step(rnd, cross) and way in ways(step + 1, part):
                    ring_copy(rnd, cross, way, step + 1, part).start()
                k = k_of(step, way)
                if hand_across and (rnd == 0 or (cross == 0 and step == 4)):
                    cross_copy(rnd, k, part).start()

    def swap_right(rnd):
        for c in range(CORES):
            begin = lax.rem(chip_at(z, side) * 2 + c + lax.div(shift[rnd], LANES), 2 * RING * SIDES)
            late = jnp.where(lax.rem(begin, 2) == core, 0, 1)
            block = lax.rem(begin + late, 2 * RING * SIDES)
            row = lax.broadcasted_iota(jnp.int32, (LANES, LANES), 0) + late * LANES
            column = lax.broadcasted_iota(jnp.int32, (LANES, LANES), 1)
            hit = row == column + lax.rem(shift[rnd], LANES)
            pick = jnp.where(hit, 1.0, 0.0).astype(jnp.bfloat16)
            near = gathered[rnd][lax.div(block, 2)]
            part = jnp.dot(near, pick, preferred_element_type=jnp.float32)
            right_mine[rnd, c] = part.astype(jnp.bfloat16)
        right_copy(rnd).start()

    def contract(rnd):
        bands = rows // 2
        right_copy(rnd).wait_recv()
        for c in range(CORES):
            both = right_mine[rnd, c].astype(jnp.float32) + right_theirs[rnd, c].astype(jnp.float32)
            right[c] = both
        pairs_of = [(j, c) for j in range(2) for c in range(CORES)]
        others = jnp.concatenate(
            [right[c, pl.ds(j, bands, stride=2), :].astype(jnp.bfloat16) for j, c in pairs_of], axis=1
        )
        weight = [occupancy[j, kq_index[rnd, k_point[rnd]]] for j in range(2)]
        for w in range(2):
            scaled = jnp.concatenate(
                [total[rnd, w * CORES + c, pl.ds(j, bands, stride=2), :] * weight[j] for j, c in pairs_of],
                axis=1,
            )
            high = scaled.astype(jnp.bfloat16)
            low = (scaled - high.astype(jnp.float32)).astype(jnp.bfloat16)
            sums = sum(
                lax.dot_general(left, others, (((1,), (1,)), ((), ())), preferred_element_type=jnp.float32)
                for left in (high, low)
            )
            partial[rnd, w] = sums.reshape(partial.shape[2:])
            sum_copy(rnd, w).start()

    def spread(rnd):
        added = []
        for w in range(2):
            sum_copy(rnd, w).wait_recv()
            added.append(partial[rnd, w, :, core] + sibling_part[rnd, w])
        outgoing[rnd] = jnp.concatenate(added, axis=1).astype(jnp.bfloat16)

        def one(i, carry):
            spread_copy(rnd, i).start()
            return carry

        lax.fori_loop(0, RING * SIDES - 1 + rnd, one, 0)

    take_ring(0, 0, 1, hand_across=False)
    take_group()
    for part in range(PARTS):
        for k in (1, 2):
            cross_copy(0, k, part).start()
    take_ring(0, 0, 2)
    whole.wait()
    wrap.wait()
    mine.wait()
    for again in range(2):
        screen_arrival(again).wait_recv()
    multiply(0, (0, 0), (0, 1), (0, 2))
    take_across(0, 0)
    multiply(0, (0, 3), (0, 4), (1, 0))
    take_ring(1, 0, 1)
    take_group_across()
    multiply(1, (0, 0), (1, 0), (0, 1), (0, 2))
    take_ring(0, 0, 3)
    take_across(0, 1)
    multiply(0, (0, 5), (0, 6), (1, 1))
    take_ring(1, 0, 2)
    take_across(0, 2)
    multiply(1, (0, 3), (0, 4))
    take_ring(1, 1, 1)
    take_across(0, 3)
    multiply(0, (1, 2), (1, 3))
    multiply(1, (1, 1), (1, 2))
    take_ring(1, 0, 3)
    take_across(0, 4)
    multiply(1, (0, 5), (0, 6))
    take_ring(0, 0, 4)
    take_ring(1, 0, 4)
    take_across(0, 5)
    multiply(0, (0, 7), (1, 4), (1, 5))
    take_ring(1, 1, 2)
    take_across(0, 6)
    multiply(1, (0, 7), (1, 3), (1, 4))
    take_across(0, 7)
    multiply(0, (1, 6), (1, 7))
    swap_right(0)
    for i, k in enumerate((5, 6, 7)):
        last_rows[i] = met_rows(1, 1, k)
    contract(0)
    take_ring(1, 1, 3)
    spread(0)
    take_across(1, 7)
    swap_right(1)
    multiply(1, (1, 5), (1, 6), (1, 7), met=jnp.concatenate([last_rows[i] for i in range(3)], axis=0))
    contract(1)
    spread(1)

    def settle(i, carry):
        spread_copy(0, i).wait_recv()
        return carry

    lax.fori_loop(0, RING * SIDES - 1, settle, 0)
    chip = z * 2 + side
    own = jnp.concatenate([partial[0, w, chip, core] + sibling_part[0, w, chip] for w in range(2)], axis=0)
    result = own + jnp.sum(incoming[0, : RING * SIDES - 1].astype(jnp.float32), axis=0)
    for again in range(2):
        screen_copy(again).wait_send()
    for rnd, cross in ((0, 0), (1, 0), (1, 1)):
        for step in range(1, last_step(rnd, cross) + 1):
            for part in range(PARTS):
                for way in ways(step, part):
                    ring_copy(rnd, cross, way, step, part).wait_send()
    for part in range(PARTS):
        group_copy(part).wait_send()
        for k in range(RING):
            cross_copy(0, k, part, own=k == 0).wait_send()
        for k in (0, 7):
            cross_copy(1, k, part).wait_send()
    for rnd in range(ROUNDS):
        right_copy(rnd).wait_send()
        for w in range(2):
            sum_copy(rnd, w).wait_send()

    def sent(i, carry):
        spread_copy(0, i).wait_send()
        return carry

    lax.fori_loop(0, RING * SIDES - 1, sent, 0)

    def last(i, carry):
        spread_copy(1, i).wait()
        return carry

    lax.fori_loop(0, RING * SIDES, last, 0)
    result = result + jnp.sum(incoming[1].astype(jnp.float32), axis=0)
    bands = out.shape[1]
    for w in range(2):
        out[w] = result[w * bands : (w + 1) * bands] * (1.0 / math.sqrt(grid_count))


def per_device(pairs, screening, kq_index, umklapp, occupancy):
    rounds, k_count, band_count, summed_count, column_count = pairs.shape
    rows = band_count * summed_count
    grid_count = screening.shape[2]
    devices = grid_count // column_count
    bands = band_count // devices
    chips = RING * SIDES
    sigma = pl.pallas_call(
        kernel,
        out_shape=jax.ShapeDtypeStruct((2, bands, band_count), jnp.float32),
        in_specs=[
            pl.BlockSpec(memory_space=pl.ANY),
            pl.BlockSpec(memory_space=pl.ANY),
            pl.BlockSpec(memory_space=pl.ANY),
            pl.BlockSpec(memory_space=pl.ANY),
            pl.BlockSpec(memory_space=pl.ANY),
        ],
        out_specs=pl.BlockSpec(memory_space=pltpu.VMEM),
        scratch_shapes=[
            pltpu.VMEM((chips, rows, column_count), jnp.bfloat16),
            pltpu.VMEM((chips, rows, column_count), jnp.bfloat16),
            pltpu.VMEM((CORES, 2, devices + 1, LANES, column_count), jnp.bfloat16),
            pltpu.VMEM((ROUNDS, LANES, 2 * LANES), jnp.bfloat16),
            pltpu.VMEM((ROUNDS, 2 * CORES, rows, column_count), jnp.float32),
            pltpu.VMEM((CORES, rows, column_count), jnp.float32),
            pltpu.VMEM((ROUNDS, CORES, rows, column_count), jnp.bfloat16),
            pltpu.VMEM((ROUNDS, CORES, rows, column_count), jnp.bfloat16),
            pltpu.VMEM((ROUNDS, 2, chips, 2, bands, band_count), jnp.float32),
            pltpu.VMEM((ROUNDS, 2, chips, bands, band_count), jnp.float32),
            pltpu.VMEM((ROUNDS, chips, 2 * bands, band_count), jnp.bfloat16),
            pltpu.VMEM((ROUNDS, chips, 2 * bands, band_count), jnp.bfloat16),
            pltpu.VMEM((3, LANES, 2 * CORES * column_count), jnp.bfloat16),
            pltpu.SMEM(kq_index.shape, jnp.int32),
            pltpu.SMEM(umklapp.shape, jnp.int32),
            pltpu.SMEM(occupancy.shape[::-1], jnp.float32),
            pltpu.SemaphoreType.DMA((COUNT,)),
            pltpu.SemaphoreType.DMA((COUNT,)),
            pltpu.SemaphoreType.DMA((6,)),
        ],
        compiler_params=pltpu.CompilerParams(
            collective_id=0, has_side_effects=True, vmem_limit_bytes=62 << 20
        ),
    )(
        pairs.reshape(rounds, rows, column_count),
        screening.reshape(2, devices, LANES, column_count),
        kq_index,
        umklapp,
        occupancy.T,
    )
    return sigma[None]


def solution(mesh):
    return jax.shard_map(
        per_device,
        mesh=mesh,
        in_specs=(P(None, "kgrp", None, None, "ga"), P("kgrp", None, None, "ga"), P(), P(), P()),
        out_specs=P("kgrp", None, "ga", None),
        check_vma=False,
    )
```

```python
import functools
import math

import jax
import jax.numpy as jnp
from jax import lax
from jax.experimental import pallas as pl
from jax.experimental.pallas import tpu as pltpu
from jax.sharding import PartitionSpec as P

ROUNDS = 2
GROUPS = 16
RING = 8
SIDES = 2
CORES = 2
LANES = 128
PARTS = 2
MESH = pl.DeviceIdType.MESH

Z0 = 0
X0 = Z0 + 2 * 4 * PARTS
X1 = X0 + RING * PARTS
Y1 = X1 + 2 * PARTS
Z1 = Y1 + PARTS
C = Z1 + SIDES * 2 * 4 * PARTS
R = C + 2
S = R + ROUNDS
A = S + ROUNDS * 2
COUNT = A + ROUNDS * RING * SIDES


def kernel(
    pairs,
    screening,
    kq_index_all,
    umklapp_all,
    occupancy_all,
    out,
    all0,
    all1,
    screen,
    shift_rows,
    total,
    right,
    right_mine,
    right_theirs,
    partial,
    sibling_part,
    outgoing,
    incoming,
    last_rows,
    kq_index,
    umklapp,
    occupancy,
    send,
    recv,
    local,
):
    group = lax.axis_index("kgrp")
    place = lax.axis_index("ga")
    z = lax.div(place, 4)
    side = lax.rem(lax.div(place, 2), 2)
    core = lax.rem(place, 2)
    tiles = screening.shape[1]
    grid_count = tiles * LANES
    rows = pairs.shape[1]
    piece = rows // PARTS
    gathered = (all0, all1)

    def at(z_at, side_at, core_at):
        return z_at * 4 + side_at * 2 + core_at

    def chip_at(z_at, side_at):
        return z_at * 2 + side_at

    def along(steps):
        return lax.rem(z + steps + 2 * RING, RING)

    before = lax.rem(group + GROUPS - 1, GROUPS)
    after = lax.rem(group + 1, GROUPS)
    upward = (group, at(along(1), side, core))
    downward = (group, at(along(-1), side, core))
    across = (group, at(z, 1 - side, core))
    sibling = (group, at(z, side, 1 - core))

    def copy(source, target, index, device):
        return pltpu.make_async_remote_copy(
            src_ref=source,
            dst_ref=target,
            send_sem=send.at[index],
            recv_sem=recv.at[index],
            device_id=device,
            device_id_type=MESH,
        )

    def cut(part):
        return pl.ds(part * piece, piece)

    def z_of(k):
        steps = lax.div(k + 1, 2)
        return along(jnp.where(lax.rem(k, 2) == 1, -steps, steps))

    def k_of(step, way):
        return 2 * step - 1 + way if step < 4 else 7

    def origin(step, way):
        return along(-step if way == 0 else step)

    def ring_copy(rnd, cross, way, step, part):
        came_from = origin(step - 1, way)
        place_of = chip_at(came_from, lax.rem(side + cross, 2))
        target = gathered[rnd].at[place_of, cut(part)]
        source = pairs.at[0, cut(part)] if rnd == 0 and step == 1 else target
        index = (Z0 if rnd == 0 else Z1) + ((cross * 2 + way) * 4 + step - 1) * PARTS + part
        return copy(source, target, index, upward if way == 0 else downward)

    def ring_arrival(rnd, cross, way, step, part):
        place_of = chip_at(origin(step, way), lax.rem(side + cross, 2))
        target = gathered[rnd].at[place_of, cut(part)]
        index = (Z0 if rnd == 0 else Z1) + ((cross * 2 + way) * 4 + step - 1) * PARTS + part
        return copy(target, target, index, upward)

    def cross_copy(rnd, k, part, own=False):
        target = gathered[rnd].at[chip_at(z_of(k), side), cut(part)]
        source = pairs.at[0, cut(part)] if own else target
        return copy(source, target, (X0 + k * PARTS if rnd == 0 else X1 + (k // 7) * PARTS) + part, across)

    def cross_arrival(rnd, k, part):
        target = gathered[rnd].at[chip_at(z_of(k), 1 - side), cut(part)]
        return copy(target, target, (X0 + k * PARTS if rnd == 0 else X1 + (k // 7) * PARTS) + part, across)

    def group_copy(part):
        target = all1.at[chip_at(z, side), cut(part)]
        return copy(pairs.at[1, cut(part)], target, Y1 + part, (before, place))

    def group_arrival(part):
        target = all1.at[chip_at(z, side), cut(part)]
        return copy(target, target, Y1 + part, sibling)

    def screen_copy(wrap):
        first, count = (tiles, 1) if wrap else (0, tiles)
        target = screen.at[core, :, pl.ds(first, count)]
        return copy(screening.at[:, pl.ds(0, count)], target, C + wrap, sibling)

    def screen_arrival(wrap):
        first, count = (tiles, 1) if wrap else (0, tiles)
        target = screen.at[1 - core, :, pl.ds(first, count)]
        return copy(target, target, C + wrap, sibling)

    def right_copy(rnd):
        return copy(right_mine.at[rnd], right_theirs.at[rnd], R + rnd, sibling)

    def sum_copy(rnd, w):
        return copy(partial.at[rnd, w, :, 1 - core], sibling_part.at[rnd, w], S + rnd * 2 + w, sibling)

    def spread_copy(rnd, i):
        turn = lax.div(i, 2)
        steps = jnp.where(lax.rem(turn, 2) == 1, 4 - lax.div(turn + 1, 2), 4 + lax.div(turn, 2))
        z_to = along(steps)
        side_to = lax.rem(side + 1 - lax.rem(i, 2), 2)
        device = (group if rnd == 0 else after, at(z_to, side_to, core))
        index = A + rnd * RING * SIDES + i
        return copy(outgoing.at[rnd, z_to * 2 + side_to], incoming.at[rnd, i], index, device)

    barrier = pltpu.get_barrier_semaphore()
    for device in (
        upward,
        downward,
        across,
        sibling,
        (after, place),
    ):
        pl.semaphore_signal(barrier, inc=1, device_id=device, device_id_type=MESH)
    whole = pltpu.make_async_copy(screening, screen.at[core, :, pl.ds(0, tiles)], local.at[0])
    whole.start()
    wrap = pltpu.make_async_copy(screening.at[:, pl.ds(0, 1)], screen.at[core, :, pl.ds(tiles, 1)], local.at[1])
    wrap.start()
    mine = pltpu.make_async_copy(pairs.at[0], all0.at[chip_at(z, side)], local.at[2])
    mine.start()
    tables = [
        pltpu.make_async_copy(source, target, local.at[3 + i])
        for i, (source, target) in enumerate(
            ((kq_index_all, kq_index), (umklapp_all, umklapp), (occupancy_all, occupancy))
        )
    ]
    for table in tables:
        table.start()
    pl.semaphore_wait(barrier, 5)

    for part in range(PARTS):
        ring_copy(0, 0, 0, 1, part).start()
        ring_copy(0, 0, 1, 1, part).start()
        cross_copy(0, 0, part, own=True).start()
        group_copy(part).start()
    for again in range(2):
        screen_copy(again).start()
    for table in tables:
        table.wait()

    k_point = (group, after)
    shift = [umklapp[rnd, k_point[rnd]] for rnd in range(ROUNDS)]
    total[...] = jnp.zeros_like(total)
    for rnd in range(ROUNDS):
        column = lax.broadcasted_iota(jnp.int32, (LANES, 2 * LANES), 1)
        row = lax.broadcasted_iota(jnp.int32, (LANES, 2 * LANES), 0)
        hit = column == row + lax.rem(grid_count - shift[rnd], LANES)
        shift_rows[rnd] = jnp.where(hit, 1.0, 0.0).astype(jnp.bfloat16)

    def met_rows(rnd, cross, k):
        block = chip_at(z_of(k), lax.rem(side + cross, 2)) * 2 + core
        start = lax.rem(block * LANES + grid_count - shift[rnd], grid_count)
        tile = lax.div(start, LANES)
        near = jnp.concatenate(
            [
                jnp.concatenate([screen[c, w, tile + i] for i in range(2)], axis=0)
                for w in range(2)
                for c in range(CORES)
            ],
            axis=1,
        )
        near = jnp.dot(shift_rows[rnd], near, preferred_element_type=jnp.float32)
        return near.astype(jnp.bfloat16)

    def multiply(rnd, *blocks, met=None):
        left = [gathered[rnd][chip_at(z_of(k), lax.rem(side + cross, 2))] for cross, k in blocks]
        if met is None:
            met = jnp.concatenate([met_rows(rnd, cross, k) for cross, k in blocks], axis=0)
        product = jnp.dot(jnp.concatenate(left, axis=1), met, preferred_element_type=jnp.float32)
        for i in range(2 * CORES):
            total[rnd, i] += product[:, i * LANES : (i + 1) * LANES]

    def take_across(rnd, k):
        for part in range(PARTS):
            cross_arrival(rnd, k, part).wait_recv()

    def take_group():
        for part in range(PARTS):
            group_arrival(part).wait_recv()
            for way in range(2):
                ring_copy(1, 0, way, 1, part).start()
            cross_copy(1, 0, part).start()

    def take_group_across():
        for part in range(PARTS):
            cross_arrival(1, 0, part).wait_recv()
            for way in range(2):
                ring_copy(1, 1, way, 1, part).start()

    def last_step(rnd, cross):
        return 3 if rnd == 1 and cross == 1 else 4

    def ways(step, part):
        return (part,) if step == 4 else (0, 1)

    def take_ring(rnd, cross, step, hand_across=True):
        for part in range(PARTS):
            for way in ways(step, part):
                ring_arrival(rnd, cross, way, step, part).wait_recv()
                if step < last_step(rnd, cross) and way in ways(step + 1, part):
                    ring_copy(rnd, cross, way, step + 1, part).start()
                k = k_of(step, way)
                if hand_across and (rnd == 0 or (cross == 0 and step == 4)):
                    cross_copy(rnd, k, part).start()

    def swap_right(rnd):
        for c in range(CORES):
            begin = lax.rem(chip_at(z, side) * 2 + c + lax.div(shift[rnd], LANES), 2 * RING * SIDES)
            late = jnp.where(lax.rem(begin, 2) == core, 0, 1)
            block = lax.rem(begin + late, 2 * RING * SIDES)
            row = lax.broadcasted_iota(jnp.int32, (LANES, LANES), 0) + late * LANES
            column = lax.broadcasted_iota(jnp.int32, (LANES, LANES), 1)
            hit = row == column + lax.rem(shift[rnd], LANES)
            pick = jnp.where(hit, 1.0, 0.0).astype(jnp.bfloat16)
            near = gathered[rnd][lax.div(block, 2)]
            part = jnp.dot(near, pick, preferred_element_type=jnp.float32)
            right_mine[rnd, c] = part.astype(jnp.bfloat16)
        right_copy(rnd).start()

    def contract(rnd):
        bands = rows // 2
        right_copy(rnd).wait_recv()
        for c in range(CORES):
            both = right_mine[rnd, c].astype(jnp.float32) + right_theirs[rnd, c].astype(jnp.float32)
            right[c] = both
        pairs_of = [(j, c) for j in range(2) for c in range(CORES)]
        others = jnp.concatenate(
            [right[c, pl.ds(j, bands, stride=2), :].astype(jnp.bfloat16) for j, c in pairs_of], axis=1
        )
        weight = [occupancy[j, kq_index[rnd, k_point[rnd]]] for j in range(2)]
        for w in range(2):
            scaled = jnp.concatenate(
                [total[rnd, w * CORES + c, pl.ds(j, bands, stride=2), :] * weight[j] for j, c in pairs_of],
                axis=1,
            )
            high = scaled.astype(jnp.bfloat16)
            low = (scaled - high.astype(jnp.float32)).astype(jnp.bfloat16)
            sums = sum(
                lax.dot_general(left, others, (((1,), (1,)), ((), ())), preferred_element_type=jnp.float32)
                for left in (high, low)
            )
            partial[rnd, w] = sums.reshape(partial.shape[2:])
            sum_copy(rnd, w).start()

    def spread(rnd):
        added = []
        for w in range(2):
            sum_copy(rnd, w).wait_recv()
            added.append(partial[rnd, w, :, core] + sibling_part[rnd, w])
        outgoing[rnd] = jnp.concatenate(added, axis=1).astype(jnp.bfloat16)

        def one(i, carry):
            spread_copy(rnd, i).start()
            return carry

        lax.fori_loop(0, RING * SIDES - 1 + rnd, one, 0)

    take_ring(0, 0, 1, hand_across=False)
    take_group()
    for part in range(PARTS):
        for k in (1, 2):
            cross_copy(0, k, part).start()
    take_ring(0, 0, 2)
    whole.wait()
    wrap.wait()
    mine.wait()
    for again in range(2):
        screen_arrival(again).wait_recv()
    multiply(0, (0, 0), (0, 1), (0, 2))
    take_across(0, 0)
    multiply(0, (0, 3), (0, 4), (1, 0))
    take_ring(1, 0, 1)
    take_group_across()
    multiply(1, (0, 0), (1, 0), (0, 1), (0, 2))
    take_ring(0, 0, 3)
    take_across(0, 1)
    multiply(0, (0, 5), (0, 6), (1, 1))
    take_ring(1, 0, 2)
    take_across(0, 2)
    multiply(1, (0, 3), (0, 4))
    take_ring(1, 1, 1)
    take_across(0, 3)
    multiply(0, (1, 2), (1, 3))
    multiply(1, (1, 1), (1, 2))
    take_ring(1, 0, 3)
    take_across(0, 4)
    multiply(1, (0, 5), (0, 6))
    take_ring(0, 0, 4)
    take_ring(1, 0, 4)
    take_across(0, 5)
    multiply(0, (0, 7), (1, 4), (1, 5))
    take_ring(1, 1, 2)
    take_across(0, 6)
    multiply(1, (0, 7), (1, 3), (1, 4))
    take_across(0, 7)
    multiply(0, (1, 6), (1, 7))
    swap_right(0)
    for i, k in enumerate((5, 6, 7)):
        last_rows[i] = met_rows(1, 1, k)
    contract(0)
    take_ring(1, 1, 3)
    spread(0)
    multiply(1, (1, 5), (1, 6), met=jnp.concatenate([last_rows[i] for i in range(2)], axis=0))
    take_across(1, 7)
    swap_right(1)
    multiply(1, (1, 7), met=last_rows[2])
    contract(1)
    spread(1)

    def settle(i, carry):
        spread_copy(0, i).wait_recv()
        return carry

    lax.fori_loop(0, RING * SIDES - 1, settle, 0)
    chip = z * 2 + side
    own = jnp.concatenate([partial[0, w, chip, core] + sibling_part[0, w, chip] for w in range(2)], axis=0)
    result = own + jnp.sum(incoming[0, : RING * SIDES - 1].astype(jnp.float32), axis=0)
    for again in range(2):
        screen_copy(again).wait_send()
    for rnd, cross in ((0, 0), (1, 0), (1, 1)):
        for step in range(1, last_step(rnd, cross) + 1):
            for part in range(PARTS):
                for way in ways(step, part):
                    ring_copy(rnd, cross, way, step, part).wait_send()
    for part in range(PARTS):
        group_copy(part).wait_send()
        for k in range(RING):
            cross_copy(0, k, part, own=k == 0).wait_send()
        for k in (0, 7):
            cross_copy(1, k, part).wait_send()
    for rnd in range(ROUNDS):
        right_copy(rnd).wait_send()
        for w in range(2):
            sum_copy(rnd, w).wait_send()

    def sent(i, carry):
        spread_copy(0, i).wait_send()
        return carry

    lax.fori_loop(0, RING * SIDES - 1, sent, 0)

    def last(i, carry):
        spread_copy(1, i).wait()
        return carry

    lax.fori_loop(0, RING * SIDES, last, 0)
    result = result + jnp.sum(incoming[1].astype(jnp.float32), axis=0)
    bands = out.shape[1]
    for w in range(2):
        out[w] = result[w * bands : (w + 1) * bands] * (1.0 / math.sqrt(grid_count))


def per_device(pairs, screening, kq_index, umklapp, occupancy):
    rounds, k_count, band_count, summed_count, column_count = pairs.shape
    rows = band_count * summed_count
    grid_count = screening.shape[2]
    devices = grid_count // column_count
    bands = band_count // devices
    chips = RING * SIDES
    sigma = pl.pallas_call(
        kernel,
        out_shape=jax.ShapeDtypeStruct((2, bands, band_count), jnp.float32),
        in_specs=[
            pl.BlockSpec(memory_space=pl.ANY),
            pl.BlockSpec(memory_space=pl.ANY),
            pl.BlockSpec(memory_space=pl.ANY),
            pl.BlockSpec(memory_space=pl.ANY),
            pl.BlockSpec(memory_space=pl.ANY),
        ],
        out_specs=pl.BlockSpec(memory_space=pltpu.VMEM),
        scratch_shapes=[
            pltpu.VMEM((chips, rows, column_count), jnp.bfloat16),
            pltpu.VMEM((chips, rows, column_count), jnp.bfloat16),
            pltpu.VMEM((CORES, 2, devices + 1, LANES, column_count), jnp.bfloat16),
            pltpu.VMEM((ROUNDS, LANES, 2 * LANES), jnp.bfloat16),
            pltpu.VMEM((ROUNDS, 2 * CORES, rows, column_count), jnp.float32),
            pltpu.VMEM((CORES, rows, column_count), jnp.float32),
            pltpu.VMEM((ROUNDS, CORES, rows, column_count), jnp.bfloat16),
            pltpu.VMEM((ROUNDS, CORES, rows, column_count), jnp.bfloat16),
            pltpu.VMEM((ROUNDS, 2, chips, 2, bands, band_count), jnp.float32),
            pltpu.VMEM((ROUNDS, 2, chips, bands, band_count), jnp.float32),
            pltpu.VMEM((ROUNDS, chips, 2 * bands, band_count), jnp.bfloat16),
            pltpu.VMEM((ROUNDS, chips, 2 * bands, band_count), jnp.bfloat16),
            pltpu.VMEM((3, LANES, 2 * CORES * column_count), jnp.bfloat16),
            pltpu.SMEM(kq_index.shape, jnp.int32),
            pltpu.SMEM(umklapp.shape, jnp.int32),
            pltpu.SMEM(occupancy.shape[::-1], jnp.float32),
            pltpu.SemaphoreType.DMA((COUNT,)),
            pltpu.SemaphoreType.DMA((COUNT,)),
            pltpu.SemaphoreType.DMA((6,)),
        ],
        compiler_params=pltpu.CompilerParams(
            collective_id=0, has_side_effects=True, vmem_limit_bytes=62 << 20
        ),
    )(
        pairs.reshape(rounds, rows, column_count),
        screening.reshape(2, devices, LANES, column_count),
        kq_index,
        umklapp,
        occupancy.T,
    )
    return sigma[None]


def solution(mesh):
    return jax.shard_map(
        per_device,
        mesh=mesh,
        in_specs=(P(None, "kgrp", None, None, "ga"), P("kgrp", None, None, "ga"), P(), P(), P()),
        out_specs=P("kgrp", None, "ga", None),
        check_vma=False,
    )
```

```python
import functools
import math

import jax
import jax.numpy as jnp
from jax import lax
from jax.experimental import pallas as pl
from jax.experimental.pallas import tpu as pltpu
from jax.sharding import PartitionSpec as P

ROUNDS = 2
GROUPS = 16
RING = 8
SIDES = 2
CORES = 2
LANES = 128
PARTS = 2
MESH = pl.DeviceIdType.MESH

Z0 = 0
X0 = Z0 + 2 * 4 * PARTS
X1 = X0 + RING * PARTS
Y1 = X1 + 2 * PARTS
Z1 = Y1 + PARTS
C = Z1 + SIDES * 2 * 4 * PARTS
R = C + 2
S = R + ROUNDS
A = S + ROUNDS * 2
COUNT = A + ROUNDS * RING * SIDES


def kernel(
    pairs,
    screening,
    kq_index_all,
    umklapp_all,
    occupancy_all,
    out,
    all0,
    all1,
    screen,
    shift_rows,
    total,
    right,
    right_mine,
    right_theirs,
    partial,
    sibling_part,
    outgoing,
    incoming,
    last_rows,
    kq_index,
    umklapp,
    occupancy,
    send,
    recv,
    local,
):
    group = lax.axis_index("kgrp")
    place = lax.axis_index("ga")
    z = lax.div(place, 4)
    side = lax.rem(lax.div(place, 2), 2)
    core = lax.rem(place, 2)
    tiles = screening.shape[1]
    grid_count = tiles * LANES
    rows = pairs.shape[1]
    piece = rows // PARTS
    gathered = (all0, all1)

    def at(z_at, side_at, core_at):
        return z_at * 4 + side_at * 2 + core_at

    def chip_at(z_at, side_at):
        return z_at * 2 + side_at

    def along(steps):
        return lax.rem(z + steps + 2 * RING, RING)

    before = lax.rem(group + GROUPS - 1, GROUPS)
    after = lax.rem(group + 1, GROUPS)
    upward = (group, at(along(1), side, core))
    downward = (group, at(along(-1), side, core))
    across = (group, at(z, 1 - side, core))
    sibling = (group, at(z, side, 1 - core))

    def copy(source, target, index, device):
        return pltpu.make_async_remote_copy(
            src_ref=source,
            dst_ref=target,
            send_sem=send.at[index],
            recv_sem=recv.at[index],
            device_id=device,
            device_id_type=MESH,
        )

    def cut(part):
        return pl.ds(part * piece, piece)

    def z_of(k):
        steps = lax.div(k + 1, 2)
        return along(jnp.where(lax.rem(k, 2) == 1, -steps, steps))

    def k_of(step, way):
        return 2 * step - 1 + way if step < 4 else 7

    def origin(step, way):
        return along(-step if way == 0 else step)

    def ring_copy(rnd, cross, way, step, part):
        came_from = origin(step - 1, way)
        place_of = chip_at(came_from, lax.rem(side + cross, 2))
        target = gathered[rnd].at[place_of, cut(part)]
        source = pairs.at[0, cut(part)] if rnd == 0 and step == 1 else target
        index = (Z0 if rnd == 0 else Z1) + ((cross * 2 + way) * 4 + step - 1) * PARTS + part
        return copy(source, target, index, upward if way == 0 else downward)

    def ring_arrival(rnd, cross, way, step, part):
        place_of = chip_at(origin(step, way), lax.rem(side + cross, 2))
        target = gathered[rnd].at[place_of, cut(part)]
        index = (Z0 if rnd == 0 else Z1) + ((cross * 2 + way) * 4 + step - 1) * PARTS + part
        return copy(target, target, index, upward)

    def cross_copy(rnd, k, part, own=False):
        target = gathered[rnd].at[chip_at(z_of(k), side), cut(part)]
        source = pairs.at[0, cut(part)] if own else target
        return copy(source, target, (X0 + k * PARTS if rnd == 0 else X1 + (k // 7) * PARTS) + part, across)

    def cross_arrival(rnd, k, part):
        target = gathered[rnd].at[chip_at(z_of(k), 1 - side), cut(part)]
        return copy(target, target, (X0 + k * PARTS if rnd == 0 else X1 + (k // 7) * PARTS) + part, across)

    def group_copy(part):
        target = all1.at[chip_at(z, side), cut(part)]
        return copy(pairs.at[1, cut(part)], target, Y1 + part, (before, place))

    def group_arrival(part):
        target = all1.at[chip_at(z, side), cut(part)]
        return copy(target, target, Y1 + part, sibling)

    def screen_copy(wrap):
        first, count = (tiles, 1) if wrap else (0, tiles)
        target = screen.at[core, :, pl.ds(first, count)]
        return copy(screening.at[:, pl.ds(0, count)], target, C + wrap, sibling)

    def screen_arrival(wrap):
        first, count = (tiles, 1) if wrap else (0, tiles)
        target = screen.at[1 - core, :, pl.ds(first, count)]
        return copy(target, target, C + wrap, sibling)

    def right_copy(rnd):
        return copy(right_mine.at[rnd], right_theirs.at[rnd], R + rnd, sibling)

    def sum_copy(rnd, w):
        return copy(partial.at[rnd, w, :, 1 - core], sibling_part.at[rnd, w], S + rnd * 2 + w, sibling)

    def spread_copy(rnd, i):
        turn = lax.div(i, 2)
        steps = jnp.where(lax.rem(turn, 2) == 1, 4 - lax.div(turn + 1, 2), 4 + lax.div(turn, 2))
        z_to = along(steps)
        side_to = lax.rem(side + 1 - lax.rem(i, 2), 2)
        device = (group if rnd == 0 else after, at(z_to, side_to, core))
        index = A + rnd * RING * SIDES + i
        return copy(outgoing.at[rnd, z_to * 2 + side_to], incoming.at[rnd, i], index, device)

    barrier = pltpu.get_barrier_semaphore()
    for device in (
        upward,
        downward,
        across,
        sibling,
        (after, place),
    ):
        pl.semaphore_signal(barrier, inc=1, device_id=device, device_id_type=MESH)
    whole = pltpu.make_async_copy(screening, screen.at[core, :, pl.ds(0, tiles)], local.at[0])
    whole.start()
    wrap = pltpu.make_async_copy(screening.at[:, pl.ds(0, 1)], screen.at[core, :, pl.ds(tiles, 1)], local.at[1])
    wrap.start()
    mine = pltpu.make_async_copy(pairs.at[0], all0.at[chip_at(z, side)], local.at[2])
    mine.start()
    tables = [
        pltpu.make_async_copy(source, target, local.at[3 + i])
        for i, (source, target) in enumerate(
            ((kq_index_all, kq_index), (umklapp_all, umklapp), (occupancy_all, occupancy))
        )
    ]
    for table in tables:
        table.start()
    pl.semaphore_wait(barrier, 5)

    for part in range(PARTS):
        ring_copy(0, 0, 0, 1, part).start()
        ring_copy(0, 0, 1, 1, part).start()
        cross_copy(0, 0, part, own=True).start()
        group_copy(part).start()
    for table in tables:
        table.wait()

    k_point = (group, after)
    shift = [umklapp[rnd, k_point[rnd]] for rnd in range(ROUNDS)]
    total[...] = jnp.zeros_like(total)
    for rnd in range(ROUNDS):
        column = lax.broadcasted_iota(jnp.int32, (LANES, 2 * LANES), 1)
        row = lax.broadcasted_iota(jnp.int32, (LANES, 2 * LANES), 0)
        hit = column == row + lax.rem(grid_count - shift[rnd], LANES)
        shift_rows[rnd] = jnp.where(hit, 1.0, 0.0).astype(jnp.bfloat16)

    def met_rows(rnd, cross, k):
        block = chip_at(z_of(k), lax.rem(side + cross, 2)) * 2 + core
        start = lax.rem(block * LANES + grid_count - shift[rnd], grid_count)
        tile = lax.div(start, LANES)
        near = jnp.concatenate(
            [
                jnp.concatenate([screen[c, w, tile + i] for i in range(2)], axis=0)
                for w in range(2)
                for c in range(CORES)
            ],
            axis=1,
        )
        near = jnp.dot(shift_rows[rnd], near, preferred_element_type=jnp.float32)
        return near.astype(jnp.bfloat16)

    def multiply(rnd, *blocks, met=None):
        left = [gathered[rnd][chip_at(z_of(k), lax.rem(side + cross, 2))] for cross, k in blocks]
        if met is None:
            met = jnp.concatenate([met_rows(rnd, cross, k) for cross, k in blocks], axis=0)
        product = jnp.dot(jnp.concatenate(left, axis=1), met, preferred_element_type=jnp.float32)
        for i in range(2 * CORES):
            total[rnd, i] += product[:, i * LANES : (i + 1) * LANES]

    def take_across(rnd, k):
        for part in range(PARTS):
            cross_arrival(rnd, k, part).wait_recv()

    def take_group():
        for part in range(PARTS):
            group_arrival(part).wait_recv()
            for way in range(2):
                ring_copy(1, 0, way, 1, part).start()
            cross_copy(1, 0, part).start()

    def take_group_across():
        for part in range(PARTS):
            cross_arrival(1, 0, part).wait_recv()
            for way in range(2):
                ring_copy(1, 1, way, 1, part).start()

    def last_step(rnd, cross):
        return 3 if rnd == 1 and cross == 1 else 4

    def ways(step, part):
        return (part,) if step == 4 else (0, 1)

    def take_ring(rnd, cross, step, hand_across=True):
        for part in range(PARTS):
            for way in ways(step, part):
                ring_arrival(rnd, cross, way, step, part).wait_recv()
                if step < last_step(rnd, cross) and way in ways(step + 1, part):
                    ring_copy(rnd, cross, way, step + 1, part).start()
                k = k_of(step, way)
                if hand_across and (rnd == 0 or (cross == 0 and step == 4)):
                    cross_copy(rnd, k, part).start()

    def swap_right(rnd):
        for c in range(CORES):
            begin = lax.rem(chip_at(z, side) * 2 + c + lax.div(shift[rnd], LANES), 2 * RING * SIDES)
            late = jnp.where(lax.rem(begin, 2) == core, 0, 1)
            block = lax.rem(begin + late, 2 * RING * SIDES)
            row = lax.broadcasted_iota(jnp.int32, (LANES, LANES), 0) + late * LANES
            column = lax.broadcasted_iota(jnp.int32, (LANES, LANES), 1)
            hit = row == column + lax.rem(shift[rnd], LANES)
            pick = jnp.where(hit, 1.0, 0.0).astype(jnp.bfloat16)
            near = gathered[rnd][lax.div(block, 2)]
            part = jnp.dot(near, pick, preferred_element_type=jnp.float32)
            right_mine[rnd, c] = part.astype(jnp.bfloat16)
        right_copy(rnd).start()

    def contract(rnd):
        bands = rows // 2
        right_copy(rnd).wait_recv()
        for c in range(CORES):
            both = right_mine[rnd, c].astype(jnp.float32) + right_theirs[rnd, c].astype(jnp.float32)
            right[c] = both
        pairs_of = [(j, c) for j in range(2) for c in range(CORES)]
        others = jnp.concatenate(
            [right[c, pl.ds(j, bands, stride=2), :].astype(jnp.bfloat16) for j, c in pairs_of], axis=1
        )
        weight = [occupancy[j, kq_index[rnd, k_point[rnd]]] for j in range(2)]
        for w in range(2):
            scaled = jnp.concatenate(
                [total[rnd, w * CORES + c, pl.ds(j, bands, stride=2), :] * weight[j] for j, c in pairs_of],
                axis=1,
            )
            high = scaled.astype(jnp.bfloat16)
            low = (scaled - high.astype(jnp.float32)).astype(jnp.bfloat16)
            sums = sum(
                lax.dot_general(left, others, (((1,), (1,)), ((), ())), preferred_element_type=jnp.float32)
                for left in (high, low)
            )
            partial[rnd, w] = sums.reshape(partial.shape[2:])
            sum_copy(rnd, w).start()

    def spread(rnd):
        added = []
        for w in range(2):
            sum_copy(rnd, w).wait_recv()
            added.append(partial[rnd, w, :, core] + sibling_part[rnd, w])
        outgoing[rnd] = jnp.concatenate(added, axis=1).astype(jnp.bfloat16)

        def one(i, carry):
            spread_copy(rnd, i).start()
            return carry

        lax.fori_loop(0, RING * SIDES - 1 + rnd, one, 0)

    take_ring(0, 0, 1, hand_across=False)
    for again in range(2):
        screen_copy(again).start()
    take_group()
    for part in range(PARTS):
        for k in (1, 2):
            cross_copy(0, k, part).start()
    take_ring(0, 0, 2)
    whole.wait()
    wrap.wait()
    mine.wait()
    for again in range(2):
        screen_arrival(again).wait_recv()
    multiply(0, (0, 0), (0, 1), (0, 2))
    take_across(0, 0)
    multiply(0, (0, 3), (0, 4), (1, 0))
    take_ring(1, 0, 1)
    take_group_across()
    multiply(1, (0, 0), (1, 0), (0, 1), (0, 2))
    take_ring(0, 0, 3)
    take_across(0, 1)
    multiply(0, (0, 5), (0, 6), (1, 1))
    take_ring(1, 0, 2)
    take_across(0, 2)
    multiply(1, (0, 3), (0, 4))
    take_ring(1, 1, 1)
    take_across(0, 3)
    multiply(0, (1, 2), (1, 3))
    multiply(1, (1, 1), (1, 2))
    take_ring(1, 0, 3)
    take_across(0, 4)
    multiply(1, (0, 5), (0, 6))
    take_ring(0, 0, 4)
    take_ring(1, 0, 4)
    take_across(0, 5)
    multiply(0, (0, 7), (1, 4), (1, 5))
    take_ring(1, 1, 2)
    take_across(0, 6)
    multiply(1, (0, 7), (1, 3), (1, 4))
    take_across(0, 7)
    multiply(0, (1, 6), (1, 7))
    swap_right(0)
    for i, k in enumerate((5, 6, 7)):
        last_rows[i] = met_rows(1, 1, k)
    contract(0)
    take_ring(1, 1, 3)
    spread(0)
    multiply(1, (1, 5), (1, 6), met=jnp.concatenate([last_rows[i] for i in range(2)], axis=0))
    take_across(1, 7)
    swap_right(1)
    multiply(1, (1, 7), met=last_rows[2])
    contract(1)
    spread(1)

    def settle(i, carry):
        spread_copy(0, i).wait_recv()
        return carry

    lax.fori_loop(0, RING * SIDES - 1, settle, 0)
    chip = z * 2 + side
    own = jnp.concatenate([partial[0, w, chip, core] + sibling_part[0, w, chip] for w in range(2)], axis=0)
    result = own + jnp.sum(incoming[0, : RING * SIDES - 1].astype(jnp.float32), axis=0)
    for again in range(2):
        screen_copy(again).wait_send()
    for rnd, cross in ((0, 0), (1, 0), (1, 1)):
        for step in range(1, last_step(rnd, cross) + 1):
            for part in range(PARTS):
                for way in ways(step, part):
                    ring_copy(rnd, cross, way, step, part).wait_send()
    for part in range(PARTS):
        group_copy(part).wait_send()
        for k in range(RING):
            cross_copy(0, k, part, own=k == 0).wait_send()
        for k in (0, 7):
            cross_copy(1, k, part).wait_send()
    for rnd in range(ROUNDS):
        right_copy(rnd).wait_send()
        for w in range(2):
            sum_copy(rnd, w).wait_send()

    def sent(i, carry):
        spread_copy(0, i).wait_send()
        return carry

    lax.fori_loop(0, RING * SIDES - 1, sent, 0)

    def last(i, carry):
        spread_copy(1, i).wait()
        return carry

    lax.fori_loop(0, RING * SIDES, last, 0)
    result = result + jnp.sum(incoming[1].astype(jnp.float32), axis=0)
    bands = out.shape[1]
    for w in range(2):
        out[w] = result[w * bands : (w + 1) * bands] * (1.0 / math.sqrt(grid_count))


def per_device(pairs, screening, kq_index, umklapp, occupancy):
    rounds, k_count, band_count, summed_count, column_count = pairs.shape
    rows = band_count * summed_count
    grid_count = screening.shape[2]
    devices = grid_count // column_count
    bands = band_count // devices
    chips = RING * SIDES
    sigma = pl.pallas_call(
        kernel,
        out_shape=jax.ShapeDtypeStruct((2, bands, band_count), jnp.float32),
        in_specs=[
            pl.BlockSpec(memory_space=pl.ANY),
            pl.BlockSpec(memory_space=pl.ANY),
            pl.BlockSpec(memory_space=pl.ANY),
            pl.BlockSpec(memory_space=pl.ANY),
            pl.BlockSpec(memory_space=pl.ANY),
        ],
        out_specs=pl.BlockSpec(memory_space=pltpu.VMEM),
        scratch_shapes=[
            pltpu.VMEM((chips, rows, column_count), jnp.bfloat16),
            pltpu.VMEM((chips, rows, column_count), jnp.bfloat16),
            pltpu.VMEM((CORES, 2, devices + 1, LANES, column_count), jnp.bfloat16),
            pltpu.VMEM((ROUNDS, LANES, 2 * LANES), jnp.bfloat16),
            pltpu.VMEM((ROUNDS, 2 * CORES, rows, column_count), jnp.float32),
            pltpu.VMEM((CORES, rows, column_count), jnp.float32),
            pltpu.VMEM((ROUNDS, CORES, rows, column_count), jnp.bfloat16),
            pltpu.VMEM((ROUNDS, CORES, rows, column_count), jnp.bfloat16),
            pltpu.VMEM((ROUNDS, 2, chips, 2, bands, band_count), jnp.float32),
            pltpu.VMEM((ROUNDS, 2, chips, bands, band_count), jnp.float32),
            pltpu.VMEM((ROUNDS, chips, 2 * bands, band_count), jnp.bfloat16),
            pltpu.VMEM((ROUNDS, chips, 2 * bands, band_count), jnp.bfloat16),
            pltpu.VMEM((3, LANES, 2 * CORES * column_count), jnp.bfloat16),
            pltpu.SMEM(kq_index.shape, jnp.int32),
            pltpu.SMEM(umklapp.shape, jnp.int32),
            pltpu.SMEM(occupancy.shape[::-1], jnp.float32),
            pltpu.SemaphoreType.DMA((COUNT,)),
            pltpu.SemaphoreType.DMA((COUNT,)),
            pltpu.SemaphoreType.DMA((6,)),
        ],
        compiler_params=pltpu.CompilerParams(
            collective_id=0, has_side_effects=True, vmem_limit_bytes=62 << 20
        ),
    )(
        pairs.reshape(rounds, rows, column_count),
        screening.reshape(2, devices, LANES, column_count),
        kq_index,
        umklapp,
        occupancy.T,
    )
    return sigma[None]


def solution(mesh):
    return jax.shard_map(
        per_device,
        mesh=mesh,
        in_specs=(P(None, "kgrp", None, None, "ga"), P("kgrp", None, None, "ga"), P(), P(), P()),
        out_specs=P("kgrp", None, "ga", None),
        check_vma=False,
    )
```
